256 devices in a mesh: rows: 256 (over y, z, x, core).
Axes of the slice: x: 4, y: 4, z: 8, core: 2. Of those that a mesh axis runs over, the one named last changes fastest.
Arguments:
- sketch: float32 [262144, 512], P('rows'), as said below
- matrix: float32 [262144, 2048], P('rows'), may hold values from -6 to 6
Outputs:
- basis: float32 [262144, 512], P('rows')
- projection: float32 [512, 2048], P(None, 'rows')
The draws below stay inside these ranges and needn't reach their ends.
Inputs may be any that keep to these rules, and one draw needn't show every extreme that they name: `sketch`: full column rank; column scales differ.
All inputs are finite; a program needn't handle non-finite values.
Results may differ from the reference program's by a relative error of at most 0.00007.
Values sent between devices are 32-bit elements; how exact they have to be, the bound alone decides.
A program may use at most 64 MiB of HBM per device.

```python
import jax
import jax.numpy as jnp
from jax import lax

RANK = 512
COLS = 2048
ROWS = 262144


def draw_sketch(key, part):
    key = jax.random.fold_in(key, 7)
    first, second = jax.random.split(key)
    values = jax.random.normal(first, (ROWS, RANK), jnp.float32)
    position = jnp.arange(ROWS, dtype=jnp.float32) / ROWS
    row_scale = jnp.power(10.0, position)
    col_scale = jnp.power(10.0, jax.random.uniform(second, (RANK,), jnp.float32))
    return values * row_scale[:, None] * col_scale[None, :]


def levels(stream_key, shape, cuts, smallest, largest):
    loudness, own = 1.0, jax.random.fold_in(stream_key, 6)
    for dim, parts in cuts:
        heights = jnp.exp(jax.random.uniform(jax.random.fold_in(own, dim), (parts,), jnp.float32, smallest / len(cuts), largest / len(cuts)))
        loudness = loudness * jnp.repeat(heights, shape[dim] // parts).reshape([-1 if axis == dim else 1 for axis in range(len(shape))])
    return loudness


def noise(own_key, dims, width, bound, shards=(), kind=jnp.bfloat16):
    drawn = jax.random.normal(own_key, dims, jnp.float32) * width
    if len(shards) > 0:
        drawn = levels(own_key, dims, shards, -0.22, 0.18) * drawn
    return jnp.clip(drawn, min=-bound, max=bound).astype(kind)


def setup_inputs(seed: int = 0) -> dict:
    seeds = jax.random.split(jax.random.key(seed), 3)
    return {
        "sketch": draw_sketch(jax.random.fold_in(seeds[2], 71), 0),
        "matrix": noise(seeds[1], (ROWS, COLS), 1.0, 6.0, ((0, 256),), jnp.float32),
    }


def reference(sketch, matrix):
    highest = lax.Precision.HIGHEST
    gram = jnp.dot(sketch.T.astype(jnp.float32), sketch.astype(jnp.float32), precision=highest, preferred_element_type=jnp.float32) / ROWS
    lower = jnp.linalg.cholesky(gram)
    basis = lax.linalg.triangular_solve(lower, sketch, left_side=False, lower=True, transpose_a=True)
    projection = jnp.dot(basis.T.astype(jnp.float32), matrix.astype(jnp.float32), precision=highest, preferred_element_type=jnp.float32) / jnp.sqrt(jnp.float32(ROWS))
    return (basis, projection)
```

```python
import functools

import jax
import jax.numpy as jnp
from jax import lax
from jax.experimental import pallas as pl
from jax.experimental.pallas import tpu as pltpu
from jax.sharding import PartitionSpec as P

HIGHEST = lax.Precision.HIGHEST
F32, BF16 = jnp.float32, jnp.bfloat16
MESH = pl.DeviceIdType.MESH
RANK = 512
STEP = 32
BLOCKS = [(j, i) for j in range(4) for i in range(j, 4)]
A_ROWS, B_ROWS = 768, 512


def dot(a, b):
    return jnp.dot(a, b, preferred_element_type=F32)


def split2(v):
    hi = v.astype(BF16)
    return hi, (v - hi.astype(F32)).astype(BF16)


def split3(v):
    hi = v.astype(BF16)
    rest = v - hi.astype(F32)
    mid = rest.astype(BF16)
    return hi, mid, (rest - mid.astype(F32)).astype(BF16)


def exchange_kernel(
    s_hbm, m_hbm, g_ref, own_ref,
    s_v, m_v, shi, smid, slo, thi, tmid, tlo,
    p, pa_r1, pb_r1, pa_h1, pb_h1, pa_r2, pb_r2, pa_h2, pb_h2, pa_r3, pb_r3, zb,
    cta, ctb, ca_r1, cb_r1, ca_h1, cb_h1, ca_r2, cb_r2, ca_h2, cb_h2, ca_r3, cb_r3, ch3, c_z,
    ssem, rsem, lsem,
):
    me = lax.axis_index("rows")
    core, x, z, y = me % 2, (me // 2) % 4, (me // 8) % 8, me // 64
    pcore = me + 1 - 2 * core
    xs = [(x + d) % 4 for d in (1, 2, 3)]
    ys = [(y + d) % 4 for d in (1, 2, 3)]
    zs = [(z + d) % 8 for d in range(1, 8)]
    px = [me + (t - x) * 2 for t in xs]
    py = [me + (t - y) * 64 for t in ys]
    pz = [me + (t - z) * 8 for t in zs]

    barrier = pltpu.get_barrier_semaphore()
    for dev in [pcore] + px + py + pz:
        pl.semaphore_signal(barrier, inc=1, device_id=(dev,), device_id_type=MESH)

    load_s = pltpu.make_async_copy(s_hbm, s_v, lsem.at[8])
    load_s.start()
    loads = []
    for j in range(8):
        cols = pl.ds(256 * j, 256)
        load = pltpu.make_async_copy(m_hbm.at[:, cols], m_v.at[:, cols], lsem.at[j])
        load.start()
        loads.append(load)

    sends = []

    def send(src, dst, dev):
        k = len(sends)
        copy = pltpu.make_async_remote_copy(
            src_ref=src, dst_ref=dst, send_sem=ssem.at[k], recv_sem=rsem.at[k],
            device_id=(dev,), device_id_type=MESH,
        )
        copy.start()
        sends.append(copy)
        return copy

    def arrived(copies):
        for copy in copies:
            copy.wait_recv()

    def rows_at(start, size):
        return pl.ds(pl.multiple_of(start, 8), size)

    load_s.wait()
    for r in range(4):
        at = pl.ds(256 * r, 256)
        v = s_v[at, :]
        shi[at, :], smid[at, :], slo[at, :] = split3(v)
        thi[:, at], tmid[:, at], tlo[:, at] = split3(v.T)

    for half in range(2):
        at, cols = pl.ds(256 * half, 256), pl.ds(256 * half, 512 - 256 * half)
        hi, mid, lo = thi[at, :], tmid[at, :], tlo[at, :]
        rhi, rmid, rlo = shi[:, cols], smid[:, cols], slo[:, cols]
        g = (dot(hi, rlo) + dot(lo, rhi) + dot(mid, rmid)) + (dot(hi, rmid) + dot(mid, rhi)) + dot(hi, rhi)
        for k, (j, i) in enumerate(BLOCKS):
            if j // 2 == half:
                a, b = 128 * (j - 2 * half), 128 * (i - 2 * half)
                p[pl.ds(128 * k, 128), :] = g[a:a + 128, b:b + 128]

    pl.semaphore_wait(barrier, 14)

    def project(j):
        loads[j].wait()
        mhi, mlo = split2(m_v[:, pl.ds(256 * j, 256)])
        c = dot(tmid[...], mhi) + dot(thi[...], mlo) + dot(thi[...], mhi)
        ct = c.T
        for t in range(32):
            yy, zz, xx, cc = j // 2, (j % 2) * 4 + t // 8, (t // 2) % 4, t % 2
            tile = ct[8 * t:8 * t + 8, :]
            cta[pl.ds(cc * 1024 + xx * 256 + yy * 64 + zz * 8, 8), :] = tile[:, :256]
            ctb[pl.ds(cc * 1024 + yy * 256 + xx * 64 + zz * 8, 8), :] = tile[:, 256:]

    s1 = [
        send(p.at[rows_at((1 - core) * 384, 384), :], pa_r1, pcore),
        send(p.at[rows_at(A_ROWS + (1 - core) * 256, 256), :], pb_r1, pcore),
    ]
    project(0)
    project(1)
    arrived(s1)
    pa_h1[...] = p[rows_at(core * 384, 384), :] + pa_r1[...]
    pb_h1[...] = p[rows_at(A_ROWS + core * 256, 256), :] + pb_r1[...]
    s2 = [send(pa_h1.at[rows_at(xs[d] * 96, 96), :], pa_r2.at[d], px[d]) for d in range(3)]
    s2 += [send(pb_h1.at[rows_at(ys[d] * 64, 64), :], pb_r2.at[d], py[d]) for d in range(3)]
    project(2)
    project(3)
    arrived(s2)
    pa_h2[...] = pa_h1[rows_at(x * 96, 96), :] + pa_r2[0] + pa_r2[1] + pa_r2[2]
    pb_h2[...] = pb_h1[rows_at(y * 64, 64), :] + pb_r2[0] + pb_r2[1] + pb_r2[2]
    s3 = [send(pa_h2.at[rows_at(ys[d] * 24, 24), :], pa_r3.at[d], py[d]) for d in range(3)]
    s3 += [send(pb_h2.at[rows_at(xs[d] * 16, 16), :], pb_r3.at[d], px[d]) for d in range(3)]
    project(4)
    arrived(s3)
    zb[z, 0:24, :] = pa_h2[rows_at(y * 24, 24), :] + pa_r3[0] + pa_r3[1] + pa_r3[2]
    zb[z, 24:40, :] = pb_h2[rows_at(x * 16, 16), :] + pb_r3[0] + pb_r3[1] + pb_r3[2]
    s4 = [send(zb.at[z], zb.at[z], pz[d]) for d in range(7)]
    project(5)
    project(6)
    arrived(s4)
    total = zb[0]
    for k in range(1, 8):
        total = total + zb[k]
    a3 = rows_at(core * 384 + x * 96 + y * 24, 24)
    b3 = rows_at(A_ROWS + core * 256 + y * 64 + x * 16, 16)
    g_ref[a3, :] = total[:24]
    g_ref[b3, :] = total[24:]
    s5 = [send(g_ref.at[a3, :], g_ref.at[a3, :], py[d]) for d in range(3)]
    s5 += [send(g_ref.at[b3, :], g_ref.at[b3, :], px[d]) for d in range(3)]
    project(7)
    arrived(s5)
    a2 = rows_at(core * 384 + x * 96, 96)
    b2 = rows_at(A_ROWS + core * 256 + y * 64, 64)
    s6 = [send(g_ref.at[a2, :], g_ref.at[a2, :], px[d]) for d in range(3)]
    s6 += [send(g_ref.at[b2, :], g_ref.at[b2, :], py[d]) for d in range(3)]
    c1 = [
        send(cta.at[rows_at((1 - core) * 1024, 1024), :], ca_r1, pcore),
        send(ctb.at[rows_at((1 - core) * 1024, 1024), :], cb_r1, pcore),
    ]
    arrived(s6)
    a1 = rows_at(core * 384, 384)
    b1 = rows_at(A_ROWS + core * 256, 256)
    s7 = [send(g_ref.at[a1, :], g_ref.at[a1, :], pcore), send(g_ref.at[b1, :], g_ref.at[b1, :], pcore)]

    arrived(c1)
    ca_h1[...] = cta[rows_at(core * 1024, 1024), :] + ca_r1[...]
    cb_h1[...] = ctb[rows_at(core * 1024, 1024), :] + cb_r1[...]
    c2 = [send(ca_h1.at[rows_at(xs[d] * 256, 256), :], ca_r2.at[d], px[d]) for d in range(3)]
    c2 += [send(cb_h1.at[rows_at(ys[d] * 256, 256), :], cb_r2.at[d], py[d]) for d in range(3)]
    arrived(s7)
    arrived(c2)
    ca_h2[...] = ca_h1[rows_at(x * 256, 256), :] + ca_r2[0] + ca_r2[1] + ca_r2[2]
    cb_h2[...] = cb_h1[rows_at(y * 256, 256), :] + cb_r2[0] + cb_r2[1] + cb_r2[2]
    c3 = [send(ca_h2.at[rows_at(ys[d] * 64, 64), :], ca_r3.at[d], py[d]) for d in range(3)]
    c3 += [send(cb_h2.at[rows_at(xs[d] * 64, 64), :], cb_r3.at[d], px[d]) for d in range(3)]
    arrived(c3)
    ch3[:, 0:256] = ca_h2[rows_at(y * 64, 64), :] + ca_r3[0] + ca_r3[1] + ca_r3[2]
    ch3[:, 256:512] = cb_h2[rows_at(x * 64, 64), :] + cb_r3[0] + cb_r3[1] + cb_r3[2]
    c4 = [send(ch3.at[rows_at(zs[d] * 8, 8), :], c_z.at[d], pz[d]) for d in range(7)]
    arrived(c4)
    total = ch3[rows_at(z * 8, 8), :]
    for d in range(7):
        total = total + c_z[d]
    own_ref[...] = total
    for copy in sends:
        copy.wait_send()


def exchange(sketch, matrix):
    def f(*shape):
        return pltpu.VMEM(shape, F32)

    def h(*shape):
        return pltpu.VMEM(shape, BF16)

    vmem = pl.BlockSpec(memory_space=pltpu.VMEM)
    rows = sketch.shape[0]
    return pl.pallas_call(
        exchange_kernel,
        out_shape=(jax.ShapeDtypeStruct((A_ROWS + B_ROWS, 128), F32), jax.ShapeDtypeStruct((8, RANK), F32)),
        in_specs=[pl.BlockSpec(memory_space=pl.ANY)] * 2,
        out_specs=(vmem, vmem),
        scratch_shapes=[
            f(rows, RANK), f(*matrix.shape), h(rows, RANK), h(rows, RANK), h(rows, RANK),
            h(RANK, rows), h(RANK, rows), h(RANK, rows),
            f(1280, 128), f(384, 128), f(256, 128), f(384, 128), f(256, 128),
            f(3, 96, 128), f(3, 64, 128), f(96, 128), f(64, 128), f(3, 24, 128), f(3, 16, 128), f(8, 40, 128),
            f(2048, 256), f(2048, 256), f(1024, 256), f(1024, 256), f(1024, 256), f(1024, 256),
            f(3, 256, 256), f(3, 256, 256), f(256, 256), f(256, 256), f(3, 64, 256), f(3, 64, 256),
            f(64, 512), f(7, 8, 512),
            pltpu.SemaphoreType.DMA((56,)), pltpu.SemaphoreType.DMA((56,)), pltpu.SemaphoreType.DMA((9,)),
        ],
        compiler_params=pltpu.CompilerParams(collective_id=0, has_side_effects=True, vmem_limit_bytes=56 << 20),
        cost_estimate=pl.CostEstimate(flops=10_000_000_000, bytes_accessed=10 << 20, transcendentals=0),
        name="exchange",
    )(sketch, matrix)


def invert_factor(w):
    lane = lax.broadcasted_iota(jnp.int32, (8, 128), 1)
    sub = lax.broadcasted_iota(jnp.int32, (8, 128), 0)
    for k in range(RANK // STEP):
        r0 = STEP * k
        lt, off = r0 // 128, r0 % 128
        tiles = [[w[pl.ds(r0 + 8 * t, 8), pl.ds(128 * l, 128)] for l in range(4)] for t in range(4)]
        bc = {}
        for c in range(STEP):
            for t in range(c // 8, 4):
                bc[c, t] = jnp.broadcast_to(tiles[t][lt][:, off + c:off + c + 1], (8, 128))
        inside = (lane >= off) & (lane < off + STEP)
        for t in range(4):
            tiles[t][lt] = jnp.where(inside, (lane - off == sub + 8 * t).astype(F32), tiles[t][lt])
        for j in range(STEP):
            tj, sj = j // 8, j % 8
            r = lax.rsqrt(jnp.broadcast_to(bc[j, tj][sj:sj + 1, :], (8, 128)))
            col = {t: bc[j, t] * r for t in range(tj, 4)}
            row = [jnp.broadcast_to(tiles[tj][l][sj:sj + 1, :], (8, 128)) * r for l in range(4)]
            for c in range(j + 1, STEP):
                scale = jnp.broadcast_to(col[c // 8][c % 8:c % 8 + 1, :], (8, 128))
                for t in range(c // 8, 4):
                    bc[c, t] = bc[c, t] - col[t] * scale
            for t in range(tj, 4):
                if t == tj:
                    below = jnp.where(sub > sj, col[t], 0.0)
                    for l in range(4):
                        tiles[t][l] = jnp.where(sub == sj, row[l], tiles[t][l] - below * row[l])
                else:
                    for l in range(4):
                        tiles[t][l] = tiles[t][l] - col[t] * row[l]
        done = jnp.concatenate([jnp.concatenate(tiles[t], axis=1) for t in range(4)], axis=0)
        w[pl.ds(r0, STEP), :] = done
        rest = RANK - r0 - STEP
        if rest:
            update = jnp.dot(done.T[r0 + STEP:, :], done, precision=HIGHEST, preferred_element_type=F32)
            below = pl.ds(r0 + STEP, rest)
            column = lax.broadcasted_iota(jnp.int32, (rest, RANK), 1)
            w[below, :] = jnp.where((column >= r0) & (column < r0 + STEP), 0.0, w[below, :]) - update
    block_row = lax.broadcasted_iota(jnp.int32, (RANK, RANK), 0) // STEP
    block_column = lax.broadcasted_iota(jnp.int32, (RANK, RANK), 1) // STEP
    w[...] = jnp.where(block_column <= block_row, w[...], 0.0)


def factor_kernel(total_rows, g_ref, own_ref, s_ref, basis_ref, proj_ref, w):
    for k, (j, i) in enumerate(BLOCKS):
        w[pl.ds(128 * j, 128), pl.ds(128 * i, 128)] = g_ref[pl.ds(128 * k, 128), :] * (1.0 / total_rows)
        if i != j:
            w[pl.ds(128 * i, 128), pl.ds(128 * j, 128)] = jnp.zeros((128, 128), F32)
    invert_factor(w)
    wt = w[...].T
    whi, wlo = split2(wt)
    for r in range(4):
        at = pl.ds(256 * r, 256)
        hi, lo = split2(s_ref[at, :])
        basis_ref[at, :] = dot(lo, whi) + dot(hi, wlo) + dot(hi, whi)
    proj_ref[...] = jnp.dot(own_ref[...], wt, precision=HIGHEST, preferred_element_type=F32) * (float(total_rows) ** -0.5)


def factor(total_rows, gram, own, sketch):
    vmem = pl.BlockSpec(memory_space=pltpu.VMEM)
    return pl.pallas_call(
        functools.partial(factor_kernel, total_rows),
        out_shape=(jax.ShapeDtypeStruct(sketch.shape, F32), jax.ShapeDtypeStruct((8, RANK), F32)),
        in_specs=[vmem] * 3,
        out_specs=(vmem, vmem),
        scratch_shapes=[pltpu.VMEM((RANK, RANK), F32)],
        compiler_params=pltpu.CompilerParams(vmem_limit_bytes=40 << 20),
        name="factor",
    )(gram, own, sketch)


def shards(sketch, matrix):
    total_rows = sketch.shape[0] * lax.axis_size("rows")
    gram, own = exchange(sketch, matrix)
    basis, projection = factor(total_rows, gram, own, sketch)
    return basis, projection.T


def solution(mesh):
    placed = (P("rows", None), P("rows", None))
    return jax.shard_map(
        shards,
        mesh=mesh,
        in_specs=placed,
        out_specs=(P("rows", None), P(None, "rows")),
        check_vma=False,
    )
```

```python
import functools

import jax
import jax.numpy as jnp
from jax import lax
from jax.experimental import pallas as pl
from jax.experimental.pallas import tpu as pltpu
from jax.sharding import PartitionSpec as P

HIGHEST = lax.Precision.HIGHEST
F32, BF16 = jnp.float32, jnp.bfloat16
MESH = pl.DeviceIdType.MESH
RANK = 512
STEP = 32
BLOCKS = [(j, i) for j in range(4) for i in range(j, 4)]
A_ROWS, B_ROWS = 768, 512


def dot(a, b):
    return jnp.dot(a, b, preferred_element_type=F32)


def split2(v):
    hi = v.astype(BF16)
    return hi, (v - hi.astype(F32)).astype(BF16)


def split3(v):
    hi = v.astype(BF16)
    rest = v - hi.astype(F32)
    mid = rest.astype(BF16)
    return hi, mid, (rest - mid.astype(F32)).astype(BF16)


def invert_factor(w, after):
    lane = lax.broadcasted_iota(jnp.int32, (8, 128), 1)
    sub = lax.broadcasted_iota(jnp.int32, (8, 128), 0)
    for k in range(RANK // STEP):
        r0 = STEP * k
        lt, off = r0 // 128, r0 % 128
        tiles = [[w[pl.ds(r0 + 8 * t, 8), pl.ds(128 * l, 128)] for l in range(4)] for t in range(4)]
        bc = {}
        for c in range(STEP):
            for t in range(c // 8, 4):
                bc[c, t] = jnp.broadcast_to(tiles[t][lt][:, off + c:off + c + 1], (8, 128))
        inside = (lane >= off) & (lane < off + STEP)
        for t in range(4):
            tiles[t][lt] = jnp.where(inside, (lane - off == sub + 8 * t).astype(F32), tiles[t][lt])
        for j in range(STEP):
            tj, sj = j // 8, j % 8
            r = lax.rsqrt(jnp.broadcast_to(bc[j, tj][sj:sj + 1, :], (8, 128)))
            col = {t: bc[j, t] * r for t in range(tj, 4)}
            row = [jnp.broadcast_to(tiles[tj][l][sj:sj + 1, :], (8, 128)) * r for l in range(4)]
            for c in range(j + 1, STEP):
                scale = jnp.broadcast_to(col[c // 8][c % 8:c % 8 + 1, :], (8, 128))
                for t in range(c // 8, 4):
                    bc[c, t] = bc[c, t] - col[t] * scale
            for t in range(tj, 4):
                if t == tj:
                    below = jnp.where(sub > sj, col[t], 0.0)
                    for l in range(4):
                        tiles[t][l] = jnp.where(sub == sj, row[l], tiles[t][l] - below * row[l])
                else:
                    for l in range(4):
                        tiles[t][l] = tiles[t][l] - col[t] * row[l]
        done = jnp.concatenate([jnp.concatenate(tiles[t], axis=1) for t in range(4)], axis=0)
        w[pl.ds(r0, STEP), :] = done
        rest = RANK - r0 - STEP
        if rest:
            hi, mid, lo = split3(done)
            left = jnp.concatenate([hi, hi, hi, mid, mid, lo], axis=0)[:, r0 + STEP:]
            right = jnp.concatenate([hi, mid, lo, hi, mid, hi], axis=0)
            update = lax.dot_general(left, right, (((0,), (0,)), ((), ())), preferred_element_type=F32)
            below = pl.ds(r0 + STEP, rest)
            column = lax.broadcasted_iota(jnp.int32, (rest, RANK), 1)
            w[below, :] = jnp.where((column >= r0) & (column < r0 + STEP), 0.0, w[below, :]) - update
        if k in after:
            after[k]()
    block_row = lax.broadcasted_iota(jnp.int32, (RANK, RANK), 0) // STEP
    block_column = lax.broadcasted_iota(jnp.int32, (RANK, RANK), 1) // STEP
    w[...] = jnp.where(block_column <= block_row, w[...], 0.0)


def exchange_kernel(
    total_rows, s_hbm, m_hbm, w, own_ref, g_ref,
    s_v, m_v, shi, smid, slo, thi, tmid, tlo,
    p, pa_r1, pb_r1, pa_h1, pb_h1, pa_r2, pb_r2, pa_h2, pb_h2, pa_r3, pb_r3, zb,
    cta, ctb, ca_r1, cb_r1, ca_h1, cb_h1, ca_r2, cb_r2, ca_h2, cb_h2, ca_r3, cb_r3, ch3, c_z,
    ssem, rsem, lsem,
):
    me = lax.axis_index("rows")
    core, x, z, y = me % 2, (me // 2) % 4, (me // 8) % 8, me // 64
    pcore = me + 1 - 2 * core
    xs = [(x + d) % 4 for d in (1, 2, 3)]
    ys = [(y + d) % 4 for d in (1, 2, 3)]
    zs = [(z + d) % 8 for d in range(1, 8)]
    px = [me + (t - x) * 2 for t in xs]
    py = [me + (t - y) * 64 for t in ys]
    pz = [me + (t - z) * 8 for t in zs]

    barrier = pltpu.get_barrier_semaphore()
    for dev in [pcore] + px + py + pz:
        pl.semaphore_signal(barrier, inc=1, device_id=(dev,), device_id_type=MESH)

    load_s = pltpu.make_async_copy(s_hbm, s_v, lsem.at[8])
    load_s.start()
    loads = []
    for j in range(8):
        cols = pl.ds(256 * j, 256)
        load = pltpu.make_async_copy(m_hbm.at[:, cols], m_v.at[:, cols], lsem.at[j])
        load.start()
        loads.append(load)

    sends = []

    def send(src, dst, dev):
        k = len(sends)
        copy = pltpu.make_async_remote_copy(
            src_ref=src, dst_ref=dst, send_sem=ssem.at[k], recv_sem=rsem.at[k],
            device_id=(dev,), device_id_type=MESH,
        )
        copy.start()
        sends.append(copy)
        return copy

    def arrived(copies):
        for copy in copies:
            copy.wait_recv()

    def rows_at(start, size):
        return pl.ds(pl.multiple_of(start, 8), size)

    load_s.wait()
    for r in range(4):
        at = pl.ds(256 * r, 256)
        v = s_v[at, :]
        shi[at, :], smid[at, :], slo[at, :] = split3(v)
        thi[:, at], tmid[:, at], tlo[:, at] = split3(v.T)

    for half in range(2):
        at, cols = pl.ds(256 * half, 256), pl.ds(256 * half, 512 - 256 * half)
        hi, mid, lo = thi[at, :], tmid[at, :], tlo[at, :]
        rhi, rmid, rlo = shi[:, cols], smid[:, cols], slo[:, cols]
        g = (dot(hi, rlo) + dot(lo, rhi) + dot(mid, rmid)) + (dot(hi, rmid) + dot(mid, rhi)) + dot(hi, rhi)
        for k, (j, i) in enumerate(BLOCKS):
            if j // 2 == half:
                a, b = 128 * (j - 2 * half), 128 * (i - 2 * half)
                p[pl.ds(128 * k, 128), :] = g[a:a + 128, b:b + 128]

    pl.semaphore_wait(barrier, 14)

    def project(j):
        loads[j].wait()
        mhi, mlo = split2(m_v[:, pl.ds(256 * j, 256)])
        c = dot(tmid[...], mhi) + dot(thi[...], mlo) + dot(thi[...], mhi)
        ct = c.T
        for t in range(32):
            yy, zz, xx, cc = j // 2, (j % 2) * 4 + t // 8, (t // 2) % 4, t % 2
            tile = ct[8 * t:8 * t + 8, :]
            cta[pl.ds(cc * 1024 + xx * 256 + yy * 64 + zz * 8, 8), :] = tile[:, :256]
            ctb[pl.ds(cc * 1024 + yy * 256 + xx * 64 + zz * 8, 8), :] = tile[:, 256:]

    s1 = [
        send(p.at[rows_at((1 - core) * 384, 384), :], pa_r1, pcore),
        send(p.at[rows_at(A_ROWS + (1 - core) * 256, 256), :], pb_r1, pcore),
    ]
    project(0)
    project(1)
    project(2)
    arrived(s1)
    pa_h1[...] = p[rows_at(core * 384, 384), :] + pa_r1[...]
    pb_h1[...] = p[rows_at(A_ROWS + core * 256, 256), :] + pb_r1[...]
    s2 = [send(pa_h1.at[rows_at(xs[d] * 96, 96), :], pa_r2.at[d], px[d]) for d in range(3)]
    s2 += [send(pb_h1.at[rows_at(ys[d] * 64, 64), :], pb_r2.at[d], py[d]) for d in range(3)]
    project(3)
    project(4)
    project(5)
    arrived(s2)
    pa_h2[...] = pa_h1[rows_at(x * 96, 96), :] + pa_r2[0] + pa_r2[1] + pa_r2[2]
    pb_h2[...] = pb_h1[rows_at(y * 64, 64), :] + pb_r2[0] + pb_r2[1] + pb_r2[2]
    s3 = [send(pa_h2.at[rows_at(ys[d] * 24, 24), :], pa_r3.at[d], py[d]) for d in range(3)]
    s3 += [send(pb_h2.at[rows_at(xs[d] * 16, 16), :], pb_r3.at[d], px[d]) for d in range(3)]
    project(6)
    project(7)
    c1 = [
        send(cta.at[rows_at((1 - core) * 1024, 1024), :], ca_r1, pcore),
        send(ctb.at[rows_at((1 - core) * 1024, 1024), :], cb_r1, pcore),
    ]
    arrived(s3)
    zb[z, 0:24, :] = pa_h2[rows_at(y * 24, 24), :] + pa_r3[0] + pa_r3[1] + pa_r3[2]
    zb[z, 24:40, :] = pb_h2[rows_at(x * 16, 16), :] + pb_r3[0] + pb_r3[1] + pb_r3[2]
    s4 = [send(zb.at[z], zb.at[z], pz[d]) for d in range(7)]
    arrived(s4)
    total = zb[0]
    for k in range(1, 8):
        total = total + zb[k]
    a3 = rows_at(core * 384 + x * 96 + y * 24, 24)
    b3 = rows_at(A_ROWS + core * 256 + y * 64 + x * 16, 16)
    g_ref[a3, :] = total[:24]
    g_ref[b3, :] = total[24:]
    s5 = [send(g_ref.at[a3, :], g_ref.at[a3, :], py[d]) for d in range(3)]
    s5 += [send(g_ref.at[b3, :], g_ref.at[b3, :], px[d]) for d in range(3)]
    arrived(c1)
    ca_h1[...] = cta[rows_at(core * 1024, 1024), :] + ca_r1[...]
    cb_h1[...] = ctb[rows_at(core * 1024, 1024), :] + cb_r1[...]
    arrived(s5)
    a2 = rows_at(core * 384 + x * 96, 96)
    b2 = rows_at(A_ROWS + core * 256 + y * 64, 64)
    s6 = [send(g_ref.at[a2, :], g_ref.at[a2, :], px[d]) for d in range(3)]
    s6 += [send(g_ref.at[b2, :], g_ref.at[b2, :], py[d]) for d in range(3)]
    arrived(s6)
    a1 = rows_at(core * 384, 384)
    b1 = rows_at(A_ROWS + core * 256, 256)
    s7 = [send(g_ref.at[a1, :], g_ref.at[a1, :], pcore), send(g_ref.at[b1, :], g_ref.at[b1, :], pcore)]
    c2 = [send(ca_h1.at[rows_at(xs[d] * 256, 256), :], ca_r2.at[d], px[d]) for d in range(3)]
    c2 += [send(cb_h1.at[rows_at(ys[d] * 256, 256), :], cb_r2.at[d], py[d]) for d in range(3)]
    arrived(s7)
    for k, (j, i) in enumerate(BLOCKS):
        w[pl.ds(128 * j, 128), pl.ds(128 * i, 128)] = g_ref[pl.ds(128 * k, 128), :] * (1.0 / total_rows)
        if i != j:
            w[pl.ds(128 * i, 128), pl.ds(128 * j, 128)] = jnp.zeros((128, 128), F32)

    def second():
        arrived(c2)
        ca_h2[...] = ca_h1[rows_at(x * 256, 256), :] + ca_r2[0] + ca_r2[1] + ca_r2[2]
        cb_h2[...] = cb_h1[rows_at(y * 256, 256), :] + cb_r2[0] + cb_r2[1] + cb_r2[2]
        c3 = [send(ca_h2.at[rows_at(ys[d] * 64, 64), :], ca_r3.at[d], py[d]) for d in range(3)]
        c3 += [send(cb_h2.at[rows_at(xs[d] * 64, 64), :], cb_r3.at[d], px[d]) for d in range(3)]
        moving.append(c3)

    def third():
        arrived(moving.pop())
        ch3[:, 0:256] = ca_h2[rows_at(y * 64, 64), :] + ca_r3[0] + ca_r3[1] + ca_r3[2]
        ch3[:, 256:512] = cb_h2[rows_at(x * 64, 64), :] + cb_r3[0] + cb_r3[1] + cb_r3[2]
        moving.append([send(ch3.at[rows_at(zs[d] * 8, 8), :], c_z.at[d], pz[d]) for d in range(7)])

    moving = []
    invert_factor(w, {9: second, 13: third})
    arrived(moving.pop())
    total = ch3[rows_at(z * 8, 8), :]
    for d in range(7):
        total = total + c_z[d]
    own_ref[...] = total
    for copy in sends:
        copy.wait_send()


def exchange(total_rows, sketch, matrix):
    def f(*shape):
        return pltpu.VMEM(shape, F32)

    def h(*shape):
        return pltpu.VMEM(shape, BF16)

    vmem = pl.BlockSpec(memory_space=pltpu.VMEM)
    rows = sketch.shape[0]
    return pl.pallas_call(
        functools.partial(exchange_kernel, total_rows),
        out_shape=(jax.ShapeDtypeStruct((RANK, RANK), F32), jax.ShapeDtypeStruct((8, RANK), F32)),
        in_specs=[pl.BlockSpec(memory_space=pl.ANY)] * 2,
        out_specs=(vmem, vmem),
        scratch_shapes=[
            f(A_ROWS + B_ROWS, 128),
            f(rows, RANK), f(*matrix.shape), h(rows, RANK), h(rows, RANK), h(rows, RANK),
            h(RANK, rows), h(RANK, rows), h(RANK, rows),
            f(1280, 128), f(384, 128), f(256, 128), f(384, 128), f(256, 128),
            f(3, 96, 128), f(3, 64, 128), f(96, 128), f(64, 128), f(3, 24, 128), f(3, 16, 128), f(8, 40, 128),
            f(2048, 256), f(2048, 256), f(1024, 256), f(1024, 256), f(1024, 256), f(1024, 256),
            f(3, 256, 256), f(3, 256, 256), f(256, 256), f(256, 256), f(3, 64, 256), f(3, 64, 256),
            f(64, 512), f(7, 8, 512),
            pltpu.SemaphoreType.DMA((56,)), pltpu.SemaphoreType.DMA((56,)), pltpu.SemaphoreType.DMA((9,)),
        ],
        compiler_params=pltpu.CompilerParams(collective_id=0, has_side_effects=True, vmem_limit_bytes=40 << 20),
        cost_estimate=pl.CostEstimate(flops=10_000_000_000, bytes_accessed=10 << 20, transcendentals=0),
        name="exchange",
    )(sketch, matrix)


def finish_kernel(total_rows, s_ref, w_ref, own_ref, basis_ref, proj_ref, whi, wlo):
    @pl.when(pl.program_id(0) == 0)
    def _():
        wt = w_ref[...].T
        whi[...], wlo[...] = split2(wt)
        proj_ref[...] = jnp.dot(own_ref[...], wt, precision=HIGHEST, preferred_element_type=F32) * (float(total_rows) ** -0.5)

    hi, lo = split2(s_ref[...])
    basis_ref[...] = dot(lo, whi[...]) + dot(hi, wlo[...]) + dot(hi, whi[...])


def finish(total_rows, sketch, w, own):
    block = pl.BlockSpec((256, RANK), lambda r: (r, 0))
    vmem = pl.BlockSpec(memory_space=pltpu.VMEM)
    return pl.pallas_call(
        functools.partial(finish_kernel, total_rows),
        out_shape=(jax.ShapeDtypeStruct(sketch.shape, F32), jax.ShapeDtypeStruct((8, RANK), F32)),
        grid=(sketch.shape[0] // 256,),
        in_specs=[block, vmem, vmem],
        out_specs=(block, vmem),
        scratch_shapes=[pltpu.VMEM((RANK, RANK), BF16), pltpu.VMEM((RANK, RANK), BF16)],
        compiler_params=pltpu.CompilerParams(vmem_limit_bytes=16 << 20),
        name="finish",
    )(sketch, w, own)


def shards(sketch, matrix):
    total_rows = sketch.shape[0] * lax.axis_size("rows")
    w, own = exchange(total_rows, sketch, matrix)
    basis, projection = finish(total_rows, sketch, w, own)
    return basis, projection.T


def solution(mesh):
    placed = (P("rows", None), P("rows", None))
    return jax.shard_map(
        shards,
        mesh=mesh,
        in_specs=placed,
        out_specs=(P("rows", None), P(None, "rows")),
        check_vma=False,
    )
```

```python
import functools

import jax
import jax.numpy as jnp
from jax import lax
from jax.experimental import pallas as pl
from jax.experimental.pallas import tpu as pltpu
from jax.sharding import PartitionSpec as P

F32, BF16 = jnp.float32, jnp.bfloat16
MESH = pl.DeviceIdType.MESH
RANK = 512
STEP = 32
BLOCKS = [(j, i) for j in range(1, 4) for i in range(j, 4)] + [(0, i) for i in range(4)]
A_ROWS, B_ROWS = 768, 512
SENDS = 74


def dot(a, b):
    return jnp.dot(a, b, preferred_element_type=F32)


def split2(v):
    hi = v.astype(BF16)
    return hi, (v - hi.astype(F32)).astype(BF16)


def split3(v):
    hi = v.astype(BF16)
    rest = v - hi.astype(F32)
    mid = rest.astype(BF16)
    return hi, mid, (rest - mid.astype(F32)).astype(BF16)


def invert_factor(w, after):
    lane = lax.broadcasted_iota(jnp.int32, (8, 128), 1)
    sub = lax.broadcasted_iota(jnp.int32, (8, 128), 0)
    for k in range(RANK // STEP):
        r0 = STEP * k
        lt, off = r0 // 128, r0 % 128
        tiles = [[w[pl.ds(r0 + 8 * t, 8), pl.ds(128 * l, 128)] for l in range(4)] for t in range(4)]
        bc = {}
        for c in range(STEP):
            for t in range(c // 8, 4):
                bc[c, t] = jnp.broadcast_to(tiles[t][lt][:, off + c:off + c + 1], (8, 128))
        inside = (lane >= off) & (lane < off + STEP)
        for t in range(4):
            tiles[t][lt] = jnp.where(inside, (lane - off == sub + 8 * t).astype(F32), tiles[t][lt])
        for j in range(STEP):
            tj, sj = j // 8, j % 8
            r = lax.rsqrt(jnp.broadcast_to(bc[j, tj][sj:sj + 1, :], (8, 128)))
            col = {t: bc[j, t] * r for t in range(tj, 4)}
            row = [jnp.broadcast_to(tiles[tj][l][sj:sj + 1, :], (8, 128)) * r for l in range(4)]
            for c in range(j + 1, STEP):
                scale = jnp.broadcast_to(col[c // 8][c % 8:c % 8 + 1, :], (8, 128))
                for t in range(c // 8, 4):
                    bc[c, t] = bc[c, t] - col[t] * scale
            for t in range(tj, 4):
                if t == tj:
                    below = jnp.where(sub > sj, col[t], 0.0)
                    for l in range(4):
                        tiles[t][l] = jnp.where(sub == sj, row[l], tiles[t][l] - below * row[l])
                else:
                    for l in range(4):
                        tiles[t][l] = tiles[t][l] - col[t] * row[l]
        done = jnp.concatenate([jnp.concatenate(tiles[t], axis=1) for t in range(4)], axis=0)
        w[pl.ds(r0, STEP), :] = done
        rest = RANK - r0 - STEP
        if rest:
            hi, mid, lo = split3(done)
            left = jnp.concatenate([hi, hi, hi, mid, mid, lo], axis=0)[:, r0 + STEP:]
            right = jnp.concatenate([hi, mid, lo, hi, mid, hi], axis=0)
            update = lax.dot_general(left, right, (((0,), (0,)), ((), ())), preferred_element_type=F32)
            below = pl.ds(r0 + STEP, rest)
            column = lax.broadcasted_iota(jnp.int32, (rest, RANK), 1)
            w[below, :] = jnp.where((column >= r0) & (column < r0 + STEP), 0.0, w[below, :]) - update
        if k in after:
            after[k]()
    block_row = lax.broadcasted_iota(jnp.int32, (RANK, RANK), 0) // STEP
    block_column = lax.broadcasted_iota(jnp.int32, (RANK, RANK), 1) // STEP
    w[...] = jnp.where(block_column <= block_row, w[...], 0.0)


def exchange_kernel(
    total_rows, s_hbm, m_hbm, basis_ref, proj_ref, w, g_ref, whi, wlo,
    s_v, m_v, shi, smid, slo, thi, tmid, tlo,
    p, pa_r1, pb_r1, pa_h1, pb_h1, pa_r2, pb_r2, pa_h2, pb_h2, pa_r3, pb_r3, za, zb,
    ct, c_r1, c_h1, ca_r2, cb_r2, ca_h2, cb_h2, ca_r3, cb_r3, c_h3, c_r4,
    ssem, rsem, lsem,
):
    me = lax.axis_index("rows")
    core, x, z, y = me % 2, (me // 2) % 4, (me // 8) % 8, me // 64
    pcore = me + 1 - 2 * core
    xs = [(x + d) % 4 for d in (1, 2, 3)]
    ys = [(y + d) % 4 for d in (1, 2, 3)]
    zs = [(z + d) % 8 for d in range(1, 8)]
    px = [me + (t - x) * 2 for t in xs]
    py = [me + (t - y) * 64 for t in ys]
    pz = [me + (t - z) * 8 for t in zs]

    barrier = pltpu.get_barrier_semaphore()
    for dev in [pcore] + px + py + pz:
        pl.semaphore_signal(barrier, inc=1, device_id=(dev,), device_id_type=MESH)

    load_s = pltpu.make_async_copy(s_hbm, s_v, lsem.at[8])
    load_s.start()
    loads = []
    for j in range(8):
        cols = pl.ds(pl.multiple_of((ys + [y])[j // 2] * 512 + (j % 2) * 256, 256), 256)
        load = pltpu.make_async_copy(m_hbm.at[:, cols], m_v.at[:, pl.ds(256 * j, 256)], lsem.at[j])
        load.start()
        loads.append(load)

    sends = []

    def send(src, dst, dev):
        k = len(sends)
        copy = pltpu.make_async_remote_copy(
            src_ref=src, dst_ref=dst, send_sem=ssem.at[k], recv_sem=rsem.at[k],
            device_id=(dev,), device_id_type=MESH,
        )
        copy.start()
        sends.append(copy)
        return copy

    def arrived(copies):
        for copy in copies:
            copy.wait_recv()

    def rows_at(start, size):
        return pl.ds(pl.multiple_of(start, 8), size)

    load_s.wait()
    for r in range(4):
        at = pl.ds(256 * r, 256)
        v = s_v[at, :]
        shi[at, :], smid[at, :], slo[at, :] = split3(v)
        thi[:, at], tmid[:, at], tlo[:, at] = split3(v.T)

    def gram(half):
        at, cols = pl.ds(256 * half, 256), pl.ds(256 * half, 512 - 256 * half)
        hi, mid, lo = thi[at, :], tmid[at, :], tlo[at, :]
        rhi, rmid, rlo = shi[:, cols], smid[:, cols], slo[:, cols]
        g = (dot(hi, rlo) + dot(lo, rhi) + dot(mid, rmid)) + (dot(hi, rmid) + dot(mid, rhi)) + dot(hi, rhi)
        for k, (j, i) in enumerate(BLOCKS):
            if j // 2 == half:
                a, b = 128 * (j - 2 * half), 128 * (i - 2 * half)
                p[pl.ds(128 * k, 128), :] = g[a:a + 128, b:b + 128]

    def project(j):
        loads[j].wait()
        mhi, mlo = split2(m_v[:, pl.ds(256 * j, 256)])
        c = dot(tmid[...], mhi) + dot(thi[...], mlo) + dot(thi[...], mhi)
        c = c.T
        for t in range(32):
            yy, zz, xx, cc = j // 2, (j % 2) * 4 + t // 8, (t // 2) % 4, t % 2
            ct[pl.ds(cc * 1024 + yy * 256 + xx * 64 + zz * 8, 8), :] = c[8 * t:8 * t + 8, :]

    def a1():
        return [send(p.at[rows_at((1 - core) * 384, 384), :], pa_r1, pcore)]

    def b1():
        return [send(p.at[rows_at(A_ROWS + (1 - core) * 256, 256), :], pb_r1, pcore)]

    def a2():
        pa_h1[...] = p[rows_at(core * 384, 384), :] + pa_r1[...]
        return [send(pa_h1.at[rows_at(xs[d] * 96, 96), :], pa_r2.at[d], px[d]) for d in range(3)]

    def b2():
        pb_h1[...] = p[rows_at(A_ROWS + core * 256, 256), :] + pb_r1[...]
        return [send(pb_h1.at[rows_at(ys[d] * 64, 64), :], pb_r2.at[d], py[d]) for d in range(3)]

    def a3():
        pa_h2[...] = pa_h1[rows_at(x * 96, 96), :] + pa_r2[0] + pa_r2[1] + pa_r2[2]
        return [send(pa_h2.at[rows_at(ys[d] * 24, 24), :], pa_r3.at[d], py[d]) for d in range(3)]

    def b3():
        pb_h2[...] = pb_h1[rows_at(y * 64, 64), :] + pb_r2[0] + pb_r2[1] + pb_r2[2]
        return [send(pb_h2.at[rows_at(xs[d] * 16, 16), :], pb_r3.at[d], px[d]) for d in range(3)]

    def a4():
        za[z] = pa_h2[rows_at(y * 24, 24), :] + pa_r3[0] + pa_r3[1] + pa_r3[2]
        return [send(za.at[z], za.at[z], pz[d]) for d in range(7)]

    def b4():
        zb[z] = pb_h2[rows_at(x * 16, 16), :] + pb_r3[0] + pb_r3[1] + pb_r3[2]
        return [send(zb.at[z], zb.at[z], pz[d]) for d in range(7)]

    def total_of(parts):
        total = parts[0]
        for k in range(1, 8):
            total = total + parts[k]
        return total

    def spread(at, devices):
        return [send(g_ref.at[at, :], g_ref.at[at, :], dev) for dev in devices]

    def a5():
        at = rows_at(core * 384 + x * 96 + y * 24, 24)
        g_ref[at, :] = total_of(za)
        return spread(at, py)

    def b5():
        at = rows_at(A_ROWS + core * 256 + y * 64 + x * 16, 16)
        g_ref[at, :] = total_of(zb)
        return spread(at, px)

    def a6():
        return spread(rows_at(core * 384 + x * 96, 96), px)

    def b6():
        return spread(rows_at(A_ROWS + core * 256 + y * 64, 64), py)

    def a7():
        return spread(rows_at(core * 384, 384), [pcore])

    def b7():
        return spread(rows_at(A_ROWS + core * 256, 256), [pcore])

    def c1(yy):
        return [send(ct.at[rows_at((1 - core) * 1024 + yy * 256, 256), :], c_r1.at[pl.ds(yy * 256, 256), :], pcore)]

    def c_sum(yy):
        at = pl.ds(yy * 256, 256)
        c_h1[at, :] = ct[rows_at(core * 1024 + yy * 256, 256), :] + c_r1[at, :]

    def c2a(yy):
        return [
            send(c_h1.at[rows_at(yy * 256 + xs[d] * 64, 64), pl.ds(0, 256)], ca_r2.at[d, pl.ds(yy * 64, 64), :], px[d])
            for d in range(3)
        ]

    def c2b(d):
        return [send(c_h1.at[pl.ds(d * 256, 256), pl.ds(256, 256)], cb_r2.at[d], py[d])]

    def c3():
        for yy in range(4):
            at = pl.ds(yy * 64, 64)
            own = c_h1[rows_at(yy * 256 + x * 64, 64), pl.ds(0, 256)]
            ca_h2[at, :] = own + ca_r2[0, at, :] + ca_r2[1, at, :] + ca_r2[2, at, :]
        cb_h2[...] = c_h1[pl.ds(768, 256), pl.ds(256, 256)] + cb_r2[0] + cb_r2[1] + cb_r2[2]
        over_y = [send(ca_h2.at[pl.ds(d * 64, 64), :], ca_r3.at[d], py[d]) for d in range(3)]
        over_x = [send(cb_h2.at[rows_at(xs[d] * 64, 64), :], cb_r3.at[d], px[d]) for d in range(3)]
        return over_y + over_x

    def c4():
        c_h3[:, 0:256] = ca_h2[pl.ds(192, 64), :] + ca_r3[0] + ca_r3[1] + ca_r3[2]
        c_h3[:, 256:512] = cb_h2[rows_at(x * 64, 64), :] + cb_r3[0] + cb_r3[1] + cb_r3[2]
        return [send(c_h3.at[rows_at(zs[d] * 8, 8), :], c_r4.at[d], pz[d]) for d in range(7)]

    gram(0)
    pl.semaphore_wait(barrier, 14)
    b = b1()
    gram(1)
    a = a1()
    project(0)
    arrived(b)
    b = b2()
    arrived(a)
    a = a2()
    project(1)
    c = [c1(0)]
    project(2)
    project(3)
    c.append(c1(1))
    arrived(b)
    b = b3()
    arrived(a)
    a = a3()
    project(4)
    project(5)
    c.append(c1(2))
    arrived(b)
    b = b4()
    arrived(a)
    a = a4()
    over = []

    def move(yy):
        arrived(c[yy])
        c_sum(yy)
        over.extend(c2a(yy))
        if yy < 3:
            over.extend(c2b(yy))

    move(0)
    move(1)
    project(6)
    project(7)
    c.append(c1(3))
    arrived(b)
    b = b5()
    arrived(a)
    a = a5()
    arrived(b)
    b = b6()
    arrived(a)
    a = a6()
    move(2)
    move(3)
    arrived(b)
    b = b7()
    arrived(a)
    a = a7()
    for j in range(1, 4):
        w[pl.ds(128 * j, 128), :] = jnp.zeros((128, RANK), F32)
    arrived(b)
    for k in range(6, 10):
        w[pl.ds(0, 128), pl.ds(128 * BLOCKS[k][1], 128)] = g_ref[pl.ds(128 * k, 128), :] * (1.0 / total_rows)

    def take_rest():
        arrived(a)
        for k, (j, i) in enumerate(BLOCKS[:6]):
            at, cols = pl.ds(128 * j, 128), pl.ds(128 * i, 128)
            w[at, cols] = w[at, cols] + g_ref[pl.ds(128 * k, 128), :] * (1.0 / total_rows)

    moving = [over]

    def move_on(stage):
        def run():
            arrived(moving.pop())
            moving.append(stage())
        return run

    invert_factor(w, {3: take_rest, 6: move_on(c3), 11: move_on(c4)})
    def turn(r, carry):
        at = pl.ds(pl.multiple_of(r * 128, 128), 128)
        whi[:, at], wlo[:, at] = split2(w[at, :].T)
        return carry

    lax.fori_loop(0, 4, turn, 0)

    def solve(hi, lo):
        return dot(lo, whi[...]) + dot(hi, wlo[...]) + dot(hi, whi[...])

    def rows_of(r, carry):
        at = pl.ds(pl.multiple_of(256 * r, 256), 256)
        basis_ref[at, :] = solve(shi[at, :], smid[at, :])
        return carry

    lax.fori_loop(0, 4, rows_of, 0)
    arrived(moving.pop())
    total = c_h3[rows_at(z * 8, 8), :]
    for d in range(7):
        total = total + c_r4[d]
    proj_ref[...] = solve(*split2(total * (float(total_rows) ** -0.5)))
    for copy in sends:
        copy.wait_send()


def exchange(total_rows, sketch, matrix):
    def f(*shape):
        return pltpu.VMEM(shape, F32)

    def h(*shape):
        return pltpu.VMEM(shape, BF16)

    vmem = pl.BlockSpec(memory_space=pltpu.VMEM)
    rows = sketch.shape[0]
    return pl.pallas_call(
        functools.partial(exchange_kernel, total_rows),
        out_shape=(jax.ShapeDtypeStruct(sketch.shape, F32), jax.ShapeDtypeStruct((8, RANK), F32)),
        in_specs=[pl.BlockSpec(memory_space=pl.ANY)] * 2,
        out_specs=(vmem, vmem),
        scratch_shapes=[
            f(RANK, RANK), f(A_ROWS + B_ROWS, 128), h(RANK, RANK), h(RANK, RANK),
            f(rows, RANK), f(*matrix.shape), h(rows, RANK), h(rows, RANK), h(rows, RANK),
            h(RANK, rows), h(RANK, rows), h(RANK, rows),
            f(1280, 128), f(384, 128), f(256, 128), f(384, 128), f(256, 128),
            f(3, 96, 128), f(3, 64, 128), f(96, 128), f(64, 128), f(3, 24, 128), f(3, 16, 128), f(8, 24, 128), f(8, 16, 128),
            f(2048, 512), f(1024, 512), f(1024, 512),
            f(3, 256, 256), f(3, 256, 256), f(256, 256), f(256, 256), f(3, 64, 256), f(3, 64, 256),
            f(64, 512), f(7, 8, 512),
            pltpu.SemaphoreType.DMA((SENDS,)), pltpu.SemaphoreType.DMA((SENDS,)), pltpu.SemaphoreType.DMA((9,)),
        ],
        compiler_params=pltpu.CompilerParams(collective_id=0, has_side_effects=True, vmem_limit_bytes=50 << 20),
        cost_estimate=pl.CostEstimate(flops=10_000_000_000, bytes_accessed=10 << 20, transcendentals=0),
        name="exchange",
    )(sketch, matrix)


def shards(sketch, matrix):
    total_rows = sketch.shape[0] * lax.axis_size("rows")
    basis, projection = exchange(total_rows, sketch, matrix)
    return basis, projection.T


def solution(mesh):
    placed = (P("rows", None), P("rows", None))
    return jax.shard_map(
        shards,
        mesh=mesh,
        in_specs=placed,
        out_specs=(P("rows", None), P(None, "rows")),
        check_vma=False,
    )
```

```python
import functools

import jax
import jax.numpy as jnp
from jax import lax
from jax.experimental import pallas as pl
from jax.experimental.pallas import tpu as pltpu
from jax.sharding import PartitionSpec as P

F32, BF16 = jnp.float32, jnp.bfloat16
MESH = pl.DeviceIdType.MESH
RANK = 512
STEP = 32
BLOCKS = [(j, i) for j in range(1, 4) for i in range(j, 4)] + [(0, i) for i in range(4)]
A_ROWS, B_ROWS = 768, 512
SENDS = 74


def dot(a, b):
    return jnp.dot(a, b, preferred_element_type=F32)


def split2(v):
    hi = v.astype(BF16)
    return hi, (v - hi.astype(F32)).astype(BF16)


def split3(v):
    hi = v.astype(BF16)
    rest = v - hi.astype(F32)
    mid = rest.astype(BF16)
    return hi, mid, (rest - mid.astype(F32)).astype(BF16)


def invert_factor(w, after, always):
    lane = lax.broadcasted_iota(jnp.int32, (8, 128), 1)
    sub = lax.broadcasted_iota(jnp.int32, (8, 128), 0)
    def step(k):
        r0 = STEP * k
        lt, off = r0 // 128, r0 % 128
        tiles = [[w[pl.ds(r0 + 8 * t, 8), pl.ds(128 * l, 128)] for l in range(4)] for t in range(4)]
        bc = {}
        for c in range(STEP):
            for t in range(c // 8, 4):
                bc[c, t] = jnp.broadcast_to(tiles[t][lt][:, off + c:off + c + 1], (8, 128))
        inside = (lane >= off) & (lane < off + STEP)
        for t in range(4):
            tiles[t][lt] = jnp.where(inside, (lane - off == sub + 8 * t).astype(F32), tiles[t][lt])
        for j in range(STEP):
            tj, sj = j // 8, j % 8
            r = lax.rsqrt(jnp.broadcast_to(bc[j, tj][sj:sj + 1, :], (8, 128)))
            col = {t: bc[j, t] * r for t in range(tj, 4)}
            row = [jnp.broadcast_to(tiles[tj][l][sj:sj + 1, :], (8, 128)) * r for l in range(4)]
            for c in range(j + 1, STEP):
                scale = jnp.broadcast_to(col[c // 8][c % 8:c % 8 + 1, :], (8, 128))
                for t in range(c // 8, 4):
                    bc[c, t] = bc[c, t] - col[t] * scale
            for t in range(tj, 4):
                if t == tj:
                    below = jnp.where(sub > sj, col[t], 0.0)
                    for l in range(4):
                        tiles[t][l] = jnp.where(sub == sj, row[l], tiles[t][l] - below * row[l])
                else:
                    for l in range(4):
                        tiles[t][l] = tiles[t][l] - col[t] * row[l]
        done = jnp.concatenate([jnp.concatenate(tiles[t], axis=1) for t in range(4)], axis=0)
        w[pl.ds(r0, STEP), :] = done
        rest = RANK - r0 - STEP
        if rest:
            hi, mid, lo = split3(done)
            left = jnp.concatenate([hi, hi, hi, mid, mid, lo], axis=0)[:, r0 + STEP:]
            right = jnp.concatenate([hi, mid, lo, hi, mid, hi], axis=0)
            update = lax.dot_general(left, right, (((0,), (0,)), ((), ())), preferred_element_type=F32)
            below = pl.ds(r0 + STEP, rest)
            column = lax.broadcasted_iota(jnp.int32, (rest, RANK), 1)
            w[below, :] = jnp.where((column >= r0) & (column < r0 + STEP), 0.0, w[below, :]) - update
    for k in range(RANK // STEP):
        pl.when(always)(functools.partial(step, k))
        if k in after:
            after[k]()
    block_row = lax.broadcasted_iota(jnp.int32, (RANK, RANK), 0) // STEP
    block_column = lax.broadcasted_iota(jnp.int32, (RANK, RANK), 1) // STEP
    w[...] = jnp.where(block_column <= block_row, w[...], 0.0)


def exchange_kernel(
    total_rows, s_hbm, m_hbm, basis_ref, proj_ref, w, g_ref, whi, wlo,
    s_v, m_v, shi, smid, slo, thi, tmid, tlo,
    p, pa_r1, pb_r1, pa_h1, pb_h1, pa_r2, pb_r2, pa_h2, pb_h2, pa_r3, pb_r3, za, zb,
    ct, c_r1, c_h1, ca_r2, cb_r2, ca_h2, cb_h2, ca_r3, cb_r3, c_h3, c_r4,
    ssem, rsem, lsem,
):
    me = lax.axis_index("rows")
    core, x, z, y = me % 2, (me // 2) % 4, (me // 8) % 8, me // 64
    pcore = me + 1 - 2 * core
    xs = [(x + d) % 4 for d in (1, 2, 3)]
    ys = [(y + d) % 4 for d in (1, 2, 3)]
    zs = [(z + d) % 8 for d in range(1, 8)]
    px = [me + (t - x) * 2 for t in xs]
    py = [me + (t - y) * 64 for t in ys]
    pz = [me + (t - z) * 8 for t in zs]

    barrier = pltpu.get_barrier_semaphore()
    for dev in [pcore] + px + py + pz:
        pl.semaphore_signal(barrier, inc=1, device_id=(dev,), device_id_type=MESH)

    load_s = []
    for r in range(4):
        at = pl.ds(256 * r, 256)
        load = pltpu.make_async_copy(s_hbm.at[at, :], s_v.at[at, :], lsem.at[8 + r])
        load.start()
        load_s.append(load)
    loads = []
    for j in range(8):
        cols = pl.ds(pl.multiple_of((ys + [y])[j // 2] * 512 + (j % 2) * 256, 256), 256)
        load = pltpu.make_async_copy(m_hbm.at[:, cols], m_v.at[:, pl.ds(256 * j, 256)], lsem.at[j])
        loads.append(load)

    sends = []

    def send(src, dst, dev):
        k = len(sends)
        copy = pltpu.make_async_remote_copy(
            src_ref=src, dst_ref=dst, send_sem=ssem.at[k], recv_sem=rsem.at[k],
            device_id=(dev,), device_id_type=MESH,
        )
        copy.start()
        sends.append(copy)
        return copy

    def arrived(copies):
        for copy in copies:
            copy.wait_recv()

    def rows_at(start, size):
        return pl.ds(pl.multiple_of(start, 8), size)

    for r in range(4):
        at = pl.ds(256 * r, 256)
        load_s[r].wait()
        if r == 3:
            for load in loads:
                load.start()
        v = s_v[at, :]
        shi[at, :], smid[at, :], slo[at, :] = split3(v)
        thi[:, at], tmid[:, at], tlo[:, at] = split3(v.T)

    def gram(half):
        at, cols = pl.ds(256 * half, 256), pl.ds(256 * half, 512 - 256 * half)
        hi, mid, lo = thi[at, :], tmid[at, :], tlo[at, :]
        rhi, rmid, rlo = shi[:, cols], smid[:, cols], slo[:, cols]
        g = (dot(hi, rlo) + dot(lo, rhi) + dot(mid, rmid)) + (dot(hi, rmid) + dot(mid, rhi)) + dot(hi, rhi)
        for k, (j, i) in enumerate(BLOCKS):
            if j // 2 == half:
                a, b = 128 * (j - 2 * half), 128 * (i - 2 * half)
                p[pl.ds(128 * k, 128), :] = g[a:a + 128, b:b + 128]

    def project(j):
        loads[j].wait()
        mhi, mlo = split2(m_v[:, pl.ds(256 * j, 256)])
        c = dot(tmid[...], mhi) + dot(thi[...], mlo) + dot(thi[...], mhi)
        c = c.T
        for t in range(32):
            yy, zz, xx, cc = j // 2, (j % 2) * 4 + t // 8, (t // 2) % 4, t % 2
            ct[pl.ds(cc * 1024 + yy * 256 + xx * 64 + zz * 8, 8), :] = c[8 * t:8 * t + 8, :]

    def a1():
        return [send(p.at[rows_at((1 - core) * 384, 384), :], pa_r1, pcore)]

    def b1():
        return [send(p.at[rows_at(A_ROWS + (1 - core) * 256, 256), :], pb_r1, pcore)]

    def a2():
        pa_h1[...] = p[rows_at(core * 384, 384), :] + pa_r1[...]
        return [send(pa_h1.at[rows_at(xs[d] * 96, 96), :], pa_r2.at[d], px[d]) for d in range(3)]

    def b2():
        pb_h1[...] = p[rows_at(A_ROWS + core * 256, 256), :] + pb_r1[...]
        return [send(pb_h1.at[rows_at(ys[d] * 64, 64), :], pb_r2.at[d], py[d]) for d in range(3)]

    def a3():
        pa_h2[...] = pa_h1[rows_at(x * 96, 96), :] + pa_r2[0] + pa_r2[1] + pa_r2[2]
        return [send(pa_h2.at[rows_at(ys[d] * 24, 24), :], pa_r3.at[d], py[d]) for d in range(3)]

    def b3():
        pb_h2[...] = pb_h1[rows_at(y * 64, 64), :] + pb_r2[0] + pb_r2[1] + pb_r2[2]
        return [send(pb_h2.at[rows_at(xs[d] * 16, 16), :], pb_r3.at[d], px[d]) for d in range(3)]

    def a4():
        za[z] = pa_h2[rows_at(y * 24, 24), :] + pa_r3[0] + pa_r3[1] + pa_r3[2]
        return [send(za.at[z], za.at[z], pz[d]) for d in range(7)]

    def b4():
        zb[z] = pb_h2[rows_at(x * 16, 16), :] + pb_r3[0] + pb_r3[1] + pb_r3[2]
        return [send(zb.at[z], zb.at[z], pz[d]) for d in range(7)]

    def total_of(parts):
        total = parts[0]
        for k in range(1, 8):
            total = total + parts[k]
        return total

    def spread(at, devices):
        return [send(g_ref.at[at, :], g_ref.at[at, :], dev) for dev in devices]

    def a5():
        at = rows_at(core * 384 + x * 96 + y * 24, 24)
        g_ref[at, :] = total_of(za)
        return spread(at, py)

    def b5():
        at = rows_at(A_ROWS + core * 256 + y * 64 + x * 16, 16)
        g_ref[at, :] = total_of(zb)
        return spread(at, px)

    def a6():
        return spread(rows_at(core * 384 + x * 96, 96), px)

    def b6():
        return spread(rows_at(A_ROWS + core * 256 + y * 64, 64), py)

    def a7():
        return spread(rows_at(core * 384, 384), [pcore])

    def b7():
        return spread(rows_at(A_ROWS + core * 256, 256), [pcore])

    def c1(yy):
        return [send(ct.at[rows_at((1 - core) * 1024 + yy * 256, 256), :], c_r1.at[pl.ds(yy * 256, 256), :], pcore)]

    def c_sum(yy):
        at = pl.ds(yy * 256, 256)
        c_h1[at, :] = ct[rows_at(core * 1024 + yy * 256, 256), :] + c_r1[at, :]

    def c2a(yy):
        return [
            send(c_h1.at[rows_at(yy * 256 + xs[d] * 64, 64), pl.ds(0, 256)], ca_r2.at[d, pl.ds(yy * 64, 64), :], px[d])
            for d in range(3)
        ]

    def c2b(d):
        return [send(c_h1.at[pl.ds(d * 256, 256), pl.ds(256, 256)], cb_r2.at[d], py[d])]

    def c3():
        for yy in range(4):
            at = pl.ds(yy * 64, 64)
            own = c_h1[rows_at(yy * 256 + x * 64, 64), pl.ds(0, 256)]
            ca_h2[at, :] = own + ca_r2[0, at, :] + ca_r2[1, at, :] + ca_r2[2, at, :]
        cb_h2[...] = c_h1[pl.ds(768, 256), pl.ds(256, 256)] + cb_r2[0] + cb_r2[1] + cb_r2[2]
        over_y = [send(ca_h2.at[pl.ds(d * 64, 64), :], ca_r3.at[d], py[d]) for d in range(3)]
        over_x = [send(cb_h2.at[rows_at(xs[d] * 64, 64), :], cb_r3.at[d], px[d]) for d in range(3)]
        return over_y + over_x

    def c4():
        c_h3[:, 0:256] = ca_h2[pl.ds(192, 64), :] + ca_r3[0] + ca_r3[1] + ca_r3[2]
        c_h3[:, 256:512] = cb_h2[rows_at(x * 64, 64), :] + cb_r3[0] + cb_r3[1] + cb_r3[2]
        return [send(c_h3.at[rows_at(zs[d] * 8, 8), :], c_r4.at[d], pz[d]) for d in range(7)]

    gram(0)
    pl.semaphore_wait(barrier, 14)
    b = b1()
    gram(1)
    a = a1()
    project(0)
    arrived(b)
    b = b2()
    arrived(a)
    a = a2()
    project(1)
    c = [c1(0)]
    project(2)
    project(3)
    c.append(c1(1))
    arrived(b)
    b = b3()
    arrived(a)
    a = a3()
    over = []

    def move(yy):
        arrived(c[yy])
        c_sum(yy)
        over.extend(c2a(yy))
        if yy < 3:
            over.extend(c2b(yy))

    move(0)
    project(4)
    project(5)
    c.append(c1(2))
    arrived(b)
    b = b4()
    arrived(a)
    a = a4()
    move(1)
    project(6)
    project(7)
    c.append(c1(3))
    move(2)
    arrived(b)
    b = b5()
    arrived(a)
    a = a5()
    move(3)
    arrived(b)
    b = b6()
    arrived(a)
    a = a6()
    arrived(b)
    b = b7()
    arrived(a)
    a = a7()
    for j in range(1, 4):
        w[pl.ds(128 * j, 128), :] = jnp.zeros((128, RANK), F32)
    arrived(b)
    for k in range(6, 10):
        w[pl.ds(0, 128), pl.ds(128 * BLOCKS[k][1], 128)] = g_ref[pl.ds(128 * k, 128), :] * (1.0 / total_rows)

    def take_rest():
        arrived(a)
        for k, (j, i) in enumerate(BLOCKS[:6]):
            at, cols = pl.ds(128 * j, 128), pl.ds(128 * i, 128)
            w[at, cols] = w[at, cols] + g_ref[pl.ds(128 * k, 128), :] * (1.0 / total_rows)

    moving = [over]

    def move_on(stage):
        def run():
            arrived(moving.pop())
            moving.append(stage())
        return run

    invert_factor(w, {3: take_rest, 4: move_on(c3), 9: move_on(c4)}, me >= 0)
    def turn(r, carry):
        at = pl.ds(pl.multiple_of(r * 128, 128), 128)
        whi[:, at], wlo[:, at] = split2(w[at, :].T)
        return carry

    lax.fori_loop(0, 4, turn, 0)

    def solve(hi, lo):
        return dot(lo, whi[...]) + dot(hi, wlo[...]) + dot(hi, whi[...])

    def rows_of(r, carry):
        at = pl.ds(pl.multiple_of(256 * r, 256), 256)
        basis_ref[at, :] = solve(shi[at, :], smid[at, :])
        return carry

    lax.fori_loop(0, 4, rows_of, 0)
    arrived(moving.pop())
    total = c_h3[rows_at(z * 8, 8), :]
    for d in range(7):
        total = total + c_r4[d]
    proj_ref[...] = solve(*split2(total * (float(total_rows) ** -0.5)))
    for copy in sends:
        copy.wait_send()


def exchange(total_rows, sketch, matrix):
    def f(*shape):
        return pltpu.VMEM(shape, F32)

    def h(*shape):
        return pltpu.VMEM(shape, BF16)

    vmem = pl.BlockSpec(memory_space=pltpu.VMEM)
    rows = sketch.shape[0]
    return pl.pallas_call(
        functools.partial(exchange_kernel, total_rows),
        out_shape=(jax.ShapeDtypeStruct(sketch.shape, F32), jax.ShapeDtypeStruct((8, RANK), F32)),
        in_specs=[pl.BlockSpec(memory_space=pl.ANY)] * 2,
        out_specs=(vmem, vmem),
        scratch_shapes=[
            f(RANK, RANK), f(A_ROWS + B_ROWS, 128), h(RANK, RANK), h(RANK, RANK),
            f(rows, RANK), f(*matrix.shape), h(rows, RANK), h(rows, RANK), h(rows, RANK),
            h(RANK, rows), h(RANK, rows), h(RANK, rows),
            f(1280, 128), f(384, 128), f(256, 128), f(384, 128), f(256, 128),
            f(3, 96, 128), f(3, 64, 128), f(96, 128), f(64, 128), f(3, 24, 128), f(3, 16, 128), f(8, 24, 128), f(8, 16, 128),
            f(2048, 512), f(1024, 512), f(1024, 512),
            f(3, 256, 256), f(3, 256, 256), f(256, 256), f(256, 256), f(3, 64, 256), f(3, 64, 256),
            f(64, 512), f(7, 8, 512),
            pltpu.SemaphoreType.DMA((SENDS,)), pltpu.SemaphoreType.DMA((SENDS,)), pltpu.SemaphoreType.DMA((12,)),
        ],
        compiler_params=pltpu.CompilerParams(collective_id=0, has_side_effects=True, vmem_limit_bytes=50 << 20),
        cost_estimate=pl.CostEstimate(flops=10_000_000_000, bytes_accessed=10 << 20, transcendentals=0),
        name="exchange",
    )(sketch, matrix)


def shards(sketch, matrix):
    total_rows = sketch.shape[0] * lax.axis_size("rows")
    basis, projection = exchange(total_rows, sketch, matrix)
    return basis, projection.T


def solution(mesh):
    placed = (P("rows", None), P("rows", None))
    return jax.shard_map(
        shards,
        mesh=mesh,
        in_specs=placed,
        out_specs=(P("rows", None), P(None, "rows")),
        check_vma=False,
    )
```
